128 devices in a mesh: row: 16 (over y, x_hi, core), col: 8 (over x_lo, z).
Axes of the slice: x: 4 (x_hi: 2, x_lo: 2; x = x_hi * 2 + x_lo), y: 4, z: 4, core: 2. Of those that a mesh axis runs over, the one named last changes fastest.
Arguments:
- inputs: bfloat16 [512, 12288], P('col', 'row'), may hold values from -6 to 6
- cotangent: bfloat16 [512, 12288], P('col', 'row'), may hold values from -6 to 6
- weight_in: bfloat16 [12288, 24576], P('row', 'col'), may hold values from -0.0546875 to 0.0546875
- weight_out: bfloat16 [24576, 12288], P('col', 'row'), may hold values from -0.0390625 to 0.0390625
Outputs:
- weight_in_grad: bfloat16 [12288, 24576], P('row', 'col')
- weight_out_grad: bfloat16 [24576, 12288], P('col', 'row')
- inputs_grad: bfloat16 [512, 12288], P('col', 'row')
The draws below stay inside these ranges and needn't reach their ends.
All inputs are finite; a program needn't handle non-finite values.
Results may differ from the reference program's by a relative error of at most 0.005.
Values may be sent and summed in bfloat16 or wider, within the bound.
No kernel may reach another device: no remote copies, remote signals or barrier semaphores. Data moves between devices by JAX's collectives and lax.ppermute only.
A program may use at most 128 MiB of HBM per device.

```python
import math
import jax
import jax.numpy as jnp

D = 12288
FF = 24576
TOK = 512


def strengthened(drawn, key, source, target, shards_of, factor):
    def block_of(axis_at):
        return (jnp.arange(drawn.shape[axis_at]) // (drawn.shape[axis_at] // shards_of)).reshape((-1,) + (1,) * (drawn.ndim - 1 - axis_at))

    near = jax.random.permutation(key, shards_of)[block_of(target)]
    far = (block_of(target) + shards_of // 2) % shards_of
    return jnp.where((block_of(source) == near) | (block_of(source) == far), factor * drawn, drawn)


def steps_of(stream_key, extent, pieces, low, top_value):
    gain, own = 1.0, jax.random.fold_in(stream_key, 6)
    for dim, blocks in pieces:
        steps = jnp.exp(jax.random.uniform(jax.random.fold_in(own, dim), (blocks,), jnp.float32, low / len(pieces), top_value / len(pieces)))
        gain = gain * jnp.repeat(steps, extent[dim] // blocks).reshape([-1 if axis == dim else 1 for axis in range(len(extent))])
    return gain


def centred(own_key, dims, spread, reach, shards=(), held_as=jnp.bfloat16):
    drawn = spread * jax.random.normal(own_key, dims, jnp.float32)
    if shards:
        drawn = drawn * steps_of(own_key, dims, shards, -0.22, 0.18)
    return jnp.clip(drawn, -reach, reach).astype(held_as)


def noise_with(key, extent, width, reach, split, heavy, kind=jnp.bfloat16):
    entries = width * jax.random.normal(key, extent, jnp.float32)
    if split:
        entries = entries * steps_of(key, extent, split, -0.22, 0.18)
    return jnp.clip(strengthened(entries, jax.random.fold_in(key, 3), *heavy), -reach, reach).astype(kind)


def setup_inputs(seed: int = 0) -> dict:
    splits = jax.random.split(jax.random.key(seed), 5)
    inputs = noise_with(splits[0], (TOK, D), 1.0, 6.0, ((0, 8), (1, 16)), (1, 0, 16, 2.0))
    cotangent = noise_with(splits[1], (TOK, D), 1.0, 6.0, ((0, 8), (1, 16)), (1, 0, 16, 2.0))
    weight_in = centred(splits[2], (D, FF), D ** -0.5, 0.0546875, ((0, 16), (1, 8)))
    weight_out = centred(splits[3], (FF, D), FF ** -0.5, 0.0390625, ((0, 8), (1, 16)))
    return dict(inputs=inputs, cotangent=cotangent, weight_in=weight_in, weight_out=weight_out)


def gelu_value(v):
    inner = math.sqrt(2.0 / math.pi) * (v + 0.044715 * v * v * v)
    return 0.5 * v * (1.0 + jnp.tanh(inner))

def gelu_slope(v):
    coeff = math.sqrt(2.0 / math.pi)
    tanh_part = jnp.tanh(coeff * (v + 0.044715 * v * v * v))
    return 0.5 * (1.0 + tanh_part) + 0.5 * v * (1.0 - tanh_part * tanh_part) * coeff * (1.0 + 3.0 * 0.044715 * v * v)

def reference(inputs, cotangent, weight_in, weight_out):
    pre = jnp.dot(inputs, weight_in, preferred_element_type=jnp.float32)
    act = gelu_value(pre).astype(jnp.bfloat16)
    act_grad = jnp.dot(cotangent, weight_out.T, preferred_element_type=jnp.float32)
    pre_grad = (act_grad * gelu_slope(pre)).astype(jnp.bfloat16)
    weight_out_grad = jnp.dot(act.T, cotangent, preferred_element_type=jnp.float32).astype(jnp.bfloat16)
    weight_in_grad = jnp.dot(inputs.T, pre_grad, preferred_element_type=jnp.float32).astype(jnp.bfloat16)
    inputs_grad = jnp.dot(pre_grad, weight_in.T, preferred_element_type=jnp.float32).astype(jnp.bfloat16)
    return (weight_in_grad, weight_out_grad, inputs_grad)
```

```python
import math

import jax
import jax.numpy as jnp
from jax import lax
from jax.sharding import PartitionSpec as P

ROW = [(y, x, c) for y in range(4) for x in range(2) for c in range(2)]
COL = [(x, z) for x in range(2) for z in range(4)]


def at_row(y, x, c):
    return ((y % 4) * 2 + x % 2) * 2 + c % 2


def at_col(x, z):
    return (x % 2) * 4 + z % 4


def from_row(a, dy, dx, dc):
    return lax.ppermute(a, "row", [(at_row(y + dy, x + dx, c + dc), at_row(y, x, c)) for y, x, c in ROW])


def from_col(a, dx, dz):
    return lax.ppermute(a, "col", [(at_col(x + dx, z + dz), at_col(x, z)) for x, z in COL])


def gelu_value(v):
    inner = math.sqrt(2.0 / math.pi) * (v + 0.044715 * v * v * v)
    return 0.5 * v * (1.0 + jnp.tanh(inner))


def gelu_slope(v):
    coeff = math.sqrt(2.0 / math.pi)
    tanh_part = jnp.tanh(coeff * (v + 0.044715 * v * v * v))
    return 0.5 * (1.0 + tanh_part) + 0.5 * v * (1.0 - tanh_part * tanh_part) * coeff * (
        1.0 + 3.0 * 0.044715 * v * v
    )


def f32(a):
    return a.astype(jnp.float32)


def bf16(a):
    return a.astype(jnp.bfloat16)


def sum_y(part):
    sent = bf16(part)
    got = [from_row(sent[dy], -dy, 0, 0) for dy in (1, 3, 2)]
    return part[0] + f32(got[0]) + f32(got[1]) + f32(got[2])


def sum_x(part):
    return part[0] + f32(from_row(bf16(part[1]), 0, 1, 0))


def sum_core(part):
    return part[0] + f32(from_row(bf16(part[1]), 0, 0, 1))


def sum_row(part, y_first):
    n = part.shape[1]
    pair = sum_core(part.reshape(2, -1, n))
    if y_first:
        one = sum_y(pair.reshape(4, -1, n))
        return sum_x(one.reshape(2, -1, n))
    pair = pair.reshape(4, 2, -1, n)
    one = sum_x(jnp.stack([pair[:, 0], pair[:, 1]]))
    return sum_y(one)


def gather_row(own, y_first):
    t, n = own.shape
    if y_first:
        ys = jnp.stack([own] + [from_row(own, dy, 0, 0) for dy in (1, 2, 3)])
        both = jnp.stack([ys, from_row(ys, 0, 1, 0)], 1)
    else:
        xs = jnp.stack([own, from_row(own, 0, 1, 0)])
        both = jnp.stack([xs] + [from_row(xs, dy, 0, 0) for dy in (1, 2, 3)])
    half = both.reshape(8 * t, n)
    return jnp.concatenate([half, from_row(half, 0, 0, 1)])


def gather_col(own, direct):
    if direct:
        got = [from_col(own, dx, dz) if (dx or dz) else own for dz in range(4) for dx in range(2)]
        return jnp.concatenate(got)
    pair = jnp.concatenate([own, from_col(own, 1, 0)])
    return jnp.concatenate([pair] + [from_col(pair, 0, dz) for dz in (1, 2, 3)])


def on_device(inputs, cotangent, weight_in, weight_out):
    row = lax.axis_index("row")
    y, x, c = row // 4, (row // 2) % 2, row % 2
    rel = jnp.arange(512)
    dc, dy, dx, t = rel // 256, (rel // 64) % 4, (rel // 32) % 2, rel % 32
    order = ((((c + dc) % 2) * 4 + (y + dy) % 4) * 2 + (x + dx) % 2) * 32 + t
    to_rel = (order[:, None] == rel[None, :]).astype(jnp.bfloat16)

    def arranged(a):
        return jnp.dot(to_rel, a, preferred_element_type=jnp.float32).astype(jnp.bfloat16)

    inputs_all = arranged(gather_col(inputs, True))
    cotangent_all = arranged(gather_col(cotangent, False))
    pre = sum_row(jnp.dot(inputs_all, weight_in, preferred_element_type=jnp.float32), True)
    act = bf16(gelu_value(pre))
    act_grad = sum_row(
        lax.dot_general(
            cotangent_all, weight_out, (((1,), (1,)), ((), ())), preferred_element_type=jnp.float32
        ),
        False,
    )
    pre_grad = bf16(act_grad * gelu_slope(pre))
    act_all = gather_row(act, False)
    weight_out_grad = bf16(
        lax.dot_general(
            act_all, cotangent_all, (((0,), (0,)), ((), ())), preferred_element_type=jnp.float32
        )
    )
    grad_all = gather_row(pre_grad, True)
    input_partial = lax.dot_general(
        grad_all, weight_in, (((1,), (1,)), ((), ())), preferred_element_type=jnp.float32
    )
    weight_in_grad = bf16(
        lax.dot_general(
            inputs_all, grad_all, (((0,), (0,)), ((), ())), preferred_element_type=jnp.float32
        )
    )
    back = lax.dot_general(
        to_rel, bf16(input_partial), (((0,), (0,)), ((), ())), preferred_element_type=jnp.float32
    )
    blocks = back.reshape(4, 2, 64, -1)
    sent = bf16(blocks)
    total = blocks[0, 0]
    for dz in range(4):
        for dx in range(2):
            if dz or dx:
                total = total + f32(from_col(sent[dz, dx], dx, -dz))
    return (weight_in_grad, weight_out_grad, bf16(total))


def solution(mesh):
    return jax.shard_map(
        on_device,
        mesh=mesh,
        in_specs=(P("col", "row"), P("col", "row"), P("row", "col"), P("col", "row")),
        out_specs=(P("row", "col"), P("col", "row"), P("col", "row")),
        check_vma=False,
    )
```

```python
import functools
import math

import jax
import jax.numpy as jnp
from jax import lax
from jax.experimental import pallas as pl
from jax.experimental.pallas import tpu as pltpu
from jax.sharding import PartitionSpec as P

ROW = [(y, x, c) for y in range(4) for x in range(2) for c in range(2)]
COL = [(x, z) for x in range(2) for z in range(4)]
MIB = 1 << 20
COST = pl.CostEstimate(flops=1, bytes_accessed=1, transcendentals=0)


def at_row(y, x, c):
    return ((y % 4) * 2 + x % 2) * 2 + c % 2


def at_col(x, z):
    return (x % 2) * 4 + z % 4


def from_row(a, dy, dx, dc):
    return lax.ppermute(a, "row", [(at_row(y + dy, x + dx, c + dc), at_row(y, x, c)) for y, x, c in ROW])


def from_col(a, dx, dz):
    return lax.ppermute(a, "col", [(at_col(x + dx, z + dz), at_col(x, z)) for x, z in COL])


def gelu_value(v):
    inner = math.sqrt(2.0 / math.pi) * (v + 0.044715 * v * v * v)
    return 0.5 * v * (1.0 + jnp.tanh(inner))


def gelu_slope(v):
    coeff = math.sqrt(2.0 / math.pi)
    tanh_part = jnp.tanh(coeff * (v + 0.044715 * v * v * v))
    return 0.5 * (1.0 + tanh_part) + 0.5 * v * (1.0 - tanh_part * tanh_part) * coeff * (
        1.0 + 3.0 * 0.044715 * v * v
    )


def f32(a):
    return a.astype(jnp.float32)


def bf16(a):
    return a.astype(jnp.bfloat16)


def contract(a, b, da, db):
    return lax.dot_general(a, b, (((da,), (db,)), ((), ())), preferred_element_type=jnp.float32)


VMEM = pl.BlockSpec(memory_space=pltpu.VMEM)
SMEM = pl.BlockSpec(memory_space=pltpu.SMEM)
TILE = 512


def params(mib):
    return pltpu.CompilerParams(vmem_limit_bytes=mib * MIB)


def loaded(first, second):
    def body(first_ref, second_ref, first_out, second_out, sems):
        copies = [
            pltpu.make_async_copy(first_ref, first_out, sems.at[0]),
            pltpu.make_async_copy(second_ref, second_out, sems.at[1]),
        ]
        for copy in copies:
            copy.start()
        for copy in copies:
            copy.wait()

    return pl.pallas_call(
        body,
        in_specs=[pl.BlockSpec(memory_space=pl.ANY)] * 2,
        out_specs=[VMEM] * 2,
        out_shape=[pltpu.VMEM(first.shape, first.dtype), pltpu.VMEM(second.shape, second.dtype)],
        scratch_shapes=[pltpu.SemaphoreType.DMA((2,))],
        compiler_params=params(16),
        cost_estimate=COST,
    )(pltpu.with_memory_space_constraint(first, pltpu.HBM), pltpu.with_memory_space_constraint(second, pltpu.HBM))


def project(tokens, weight, place, hidden_dim):
    rows, k = tokens.shape
    hidden = weight.shape[hidden_dim]
    half = rows // 2

    def body(place_ref, tokens_ref, weight_ref, keep_ref, send_ref, placed_ref):
        for b in range(rows // 16):
            start = pl.multiple_of(place_ref[b] * 16, 16)
            placed_ref[pl.ds(16 * b, 16), :] = tokens_ref[pl.ds(start, 16), :]
        for i in range(hidden // TILE):
            part = pl.ds(i * TILE, TILE)
            weight_part = weight_ref[:, part] if hidden_dim == 1 else weight_ref[part, :]
            total = contract(placed_ref[...], weight_part, 1, 1 - hidden_dim)
            keep_ref[:, part] = total[:half]
            send_ref[:, part] = bf16(total[half:])

    return pl.pallas_call(
        body,
        in_specs=[SMEM, VMEM, VMEM],
        out_specs=[VMEM, VMEM, VMEM],
        out_shape=[
            pltpu.VMEM((half, hidden), jnp.float32),
            pltpu.VMEM((half, hidden), jnp.bfloat16),
            pltpu.VMEM((rows, k), jnp.bfloat16),
        ],
        compiler_params=params(16),
        cost_estimate=COST,
    )(place, tokens, weight)


def back_project(own, other, weight, place):
    p, q, _, t, hidden = own.shape
    half = p * q * t
    k = weight.shape[0]

    def body(place_ref, own_ref, other_ref, weight_ref, out_ref):
        grad = jnp.concatenate([own_ref[:, :, 1].reshape(half, hidden), other_ref[:, :, 1].reshape(half, hidden)])
        for i in range(k // 256):
            part = pl.ds(i * 256, 256)
            total = contract(grad, weight_ref[part, :], 1, 1)
            for b in range(2 * half // 16):
                start = pl.multiple_of(place_ref[b] * 16, 16)
                out_ref[pl.ds(start, 16), part] = total[16 * b : 16 * b + 16]

    return pl.pallas_call(
        body,
        in_specs=[SMEM, VMEM, VMEM, VMEM],
        out_specs=VMEM,
        out_shape=pltpu.VMEM((2 * half, k), jnp.float32),
        compiler_params=params(16),
        cost_estimate=COST,
    )(place, own, other, weight)


def weight_grad(parts, tokens, which):
    hidden = parts[0].shape[-1]
    rows, k = tokens[0].shape
    chunks = len(tokens)
    steps = hidden // TILE

    def body(*refs):
        part_refs, token_refs, out_ref = refs[: 2 * chunks], refs[2 * chunks : 3 * chunks], refs[3 * chunks]
        made, sems = refs[3 * chunks + 1 :][:2]
        both = jnp.concatenate([ref[...] for ref in token_refs])
        if which == 1:
            turned = refs[-1]
            turned[...] = both.T

        copies = []
        for i in range(steps):
            part = pl.ds(i * TILE, TILE)
            value = jnp.concatenate([ref[:, :, which, :, part].reshape(rows // 2, TILE) for ref in part_refs])
            if which == 0:
                made[i] = bf16(contract(value, both, 0, 0))
                target = out_ref.at[part, :]
            else:
                made[i] = bf16(contract(turned[...], value, 1, 0))
                target = out_ref.at[:, part]
            copies.append(pltpu.make_async_copy(made.at[i], target, sems.at[i]))
            copies[-1].start()
        for copy in copies:
            copy.wait()

    return pl.pallas_call(
        body,
        in_specs=[VMEM] * (3 * chunks),
        out_specs=pl.BlockSpec(memory_space=pl.ANY),
        out_shape=jax.ShapeDtypeStruct((hidden, k) if which == 0 else (k, hidden), jnp.bfloat16),
        scratch_shapes=[
            pltpu.VMEM((steps, TILE, k) if which == 0 else (steps, k, TILE), jnp.bfloat16),
            pltpu.SemaphoreType.DMA((steps,)),
        ]
        + ([] if which == 0 else [pltpu.VMEM((k, chunks * rows), jnp.bfloat16)]),
        compiler_params=params(16),
        cost_estimate=COST,
    )(*parts, *tokens)


def gather_y(a):
    return jnp.stack([a] + [from_row(a, dy, 0, 0) for dy in (1, 2, 3)])


def gather_x(a):
    return jnp.stack([a, from_row(a, 0, 1, 0)])


def gather_z(a):
    return jnp.stack([a] + [from_col(a, 0, dz) for dz in (1, 2, 3)])


def sum_y(part):
    got = [from_row(bf16(part(dy)), -dy, 0, 0) for dy in (1, 3, 2)]
    return part(0) + f32(got[0]) + f32(got[1]) + f32(got[2])


def sum_x(part):
    return part(0) + f32(from_row(bf16(part(1)), 0, 1, 0))


def sum_z(part):
    got = [from_col(bf16(part[dz]), 0, -dz) for dz in (1, 3, 2)]
    return part[0] + f32(got[0]) + f32(got[1]) + f32(got[2])


def tied(a, *others):
    return lax.optimization_barrier((a, *others))[0]


def on_device(inputs, cotangent, weight_in, weight_out):
    n, k = inputs.shape
    row = lax.axis_index("row")
    y, x, c = row // 4, (row // 2) % 2, row % 2

    def place_of(x_outer):
        b = jnp.arange(16, dtype=jnp.int32)
        dc = b // 8
        dx, dy = ((b // 4) % 2, b % 4) if x_outer else (b % 2, (b // 2) % 4)
        return (((y + dy) % 4) * 2 + (c + dc) % 2) * 2 + (x + dx) % 2

    def pairs_of(tokens, place, weights):
        pairs, placed = [], []
        for m in range(2):
            keep, send, rel = project(tokens[:, m].reshape(4 * n, k), weights[m], place, 1 - m)
            pairs.append(keep + f32(from_row(send, 0, 0, 1)))
            placed.append(rel)
        return jnp.stack(pairs), placed

    def made_of(sums):
        pre, act_grad = sums
        return jnp.stack([bf16(gelu_value(pre)), bf16(act_grad * gelu_slope(pre))])

    own = jnp.stack([inputs, cotangent])
    near = from_col(own, 1, 0)
    weights = loaded(tied(weight_in, near), weight_out)
    tokens_a = jnp.stack([tied(own, weights[0])] + [from_col(own, 0, dz) for dz in (1, 2, 3)])
    tokens_a, tokens_b = lax.optimization_barrier((tokens_a, gather_z(near)))
    place_a, place_b = place_of(True), place_of(False)
    pair_a, placed_a = pairs_of(tokens_a, place_a, weights)
    pair_b, placed_b = pairs_of(tokens_b, place_b, weights)
    pair_a, pair_b = pair_a.reshape(2, 2, 4, 16, -1), pair_b.reshape(2, 4, 2, 16, -1)

    one_a, one_b = sum_y(lambda dy: pair_a[:, :, dy]), sum_x(lambda dx: pair_b[:, :, dx])
    one_a, one_b = lax.optimization_barrier((one_a, one_b))
    sums_a, sums_b = sum_x(lambda dx: one_a[:, dx]), sum_y(lambda dy: one_b[:, dy])
    made_a, made_b = made_of(sums_a), made_of(sums_b)
    made_a, made_b = lax.optimization_barrier((made_a, made_b))
    part_a, part_b = lax.optimization_barrier((gather_y(made_a), gather_x(made_b)))
    half_a, half_b = gather_x(part_a), gather_y(part_b)
    other_b = from_row(half_b, 0, 0, 1)
    back_b = back_project(half_b, other_b, weights[0], place_b).reshape(4, n, k)
    other_a = from_row(half_a, 0, 0, 1)
    back_a = back_project(half_a, other_a, weights[0], place_a).reshape(4, n, k)
    total = sum_z(back_a)
    for dz in (0, 1, 3, 2):
        total = total + f32(from_col(bf16(back_b[dz]), 1, -dz))
    parts = [half_a, other_a, half_b, other_b]
    weight_out_grad = weight_grad(parts, [placed_a[1], placed_b[1]], 0)
    weight_in_grad = weight_grad(parts, [placed_a[0], placed_b[0]], 1)
    return (weight_in_grad, weight_out_grad, bf16(total))


def solution(mesh):
    return jax.shard_map(
        on_device,
        mesh=mesh,
        in_specs=(P("col", "row"), P("col", "row"), P("row", "col"), P("col", "row")),
        out_specs=(P("row", "col"), P("col", "row"), P("col", "row")),
        check_vma=False,
    )
```

```python
import functools
import math

import jax
import jax.numpy as jnp
from jax import lax
from jax.experimental import pallas as pl
from jax.experimental.pallas import tpu as pltpu
from jax.sharding import PartitionSpec as P

ROW = [(y, x, c) for y in range(4) for x in range(2) for c in range(2)]
COL = [(x, z) for x in range(2) for z in range(4)]
MIB = 1 << 20
COST = pl.CostEstimate(flops=1, bytes_accessed=1, transcendentals=0)


def at_row(y, x, c):
    return ((y % 4) * 2 + x % 2) * 2 + c % 2


def at_col(x, z):
    return (x % 2) * 4 + z % 4


def from_row(a, dy, dx, dc):
    return lax.ppermute(a, "row", [(at_row(y + dy, x + dx, c + dc), at_row(y, x, c)) for y, x, c in ROW])


def from_col(a, dx, dz):
    return lax.ppermute(a, "col", [(at_col(x + dx, z + dz), at_col(x, z)) for x, z in COL])


def gelu_value(v):
    inner = math.sqrt(2.0 / math.pi) * (v + 0.044715 * v * v * v)
    return 0.5 * v * (1.0 + jnp.tanh(inner))


def gelu_slope(v):
    coeff = math.sqrt(2.0 / math.pi)
    tanh_part = jnp.tanh(coeff * (v + 0.044715 * v * v * v))
    return 0.5 * (1.0 + tanh_part) + 0.5 * v * (1.0 - tanh_part * tanh_part) * coeff * (
        1.0 + 3.0 * 0.044715 * v * v
    )


def f32(a):
    return a.astype(jnp.float32)


def bf16(a):
    return a.astype(jnp.bfloat16)


def contract(a, b, da, db):
    return lax.dot_general(a, b, (((da,), (db,)), ((), ())), preferred_element_type=jnp.float32)


VMEM = pl.BlockSpec(memory_space=pltpu.VMEM)
SMEM = pl.BlockSpec(memory_space=pltpu.SMEM)
TILE = 512


def params(mib):
    return pltpu.CompilerParams(vmem_limit_bytes=mib * MIB)


def loaded(first, second):
    def body(first_ref, second_ref, first_out, second_out, sems):
        copies = [
            pltpu.make_async_copy(first_ref, first_out, sems.at[0]),
            pltpu.make_async_copy(second_ref, second_out, sems.at[1]),
        ]
        for copy in copies:
            copy.start()
        for copy in copies:
            copy.wait()

    return pl.pallas_call(
        body,
        in_specs=[pl.BlockSpec(memory_space=pl.ANY)] * 2,
        out_specs=[VMEM] * 2,
        out_shape=[pltpu.VMEM(first.shape, first.dtype), pltpu.VMEM(second.shape, second.dtype)],
        scratch_shapes=[pltpu.SemaphoreType.DMA((2,))],
        compiler_params=params(16),
        cost_estimate=COST,
    )(pltpu.with_memory_space_constraint(first, pltpu.HBM), pltpu.with_memory_space_constraint(second, pltpu.HBM))


def project(tokens, weights, place):
    z, _, n, k = tokens.shape
    rows = z * n
    half, hidden = rows // 2, weights[0].shape[1]

    def body(place_ref, tokens_ref, in_ref, out_ref, keep_ref, send_ref, *placed_refs):
        for m, (weight_ref, placed_ref) in enumerate(zip((in_ref, out_ref), placed_refs)):
            for b in range(rows // 16):
                at = place_ref[b]
                start = pl.multiple_of(lax.rem(at, n // 16) * 16, 16)
                placed_ref[pl.ds(16 * b, 16), :] = tokens_ref[lax.div(at, n // 16), m, pl.ds(start, 16), :]
            for i in range(hidden // TILE):
                part = pl.ds(i * TILE, TILE)
                weight_part = weight_ref[part, :] if m else weight_ref[:, part]
                total = contract(placed_ref[...], weight_part, 1, m)
                keep_ref[m, :, part] = total[:half]
                send_ref[m, :, part] = bf16(total[half:])

    return pl.pallas_call(
        body,
        in_specs=[SMEM, VMEM, VMEM, VMEM],
        out_specs=[VMEM] * 4,
        out_shape=[
            pltpu.VMEM((2, half, hidden), jnp.float32),
            pltpu.VMEM((2, half, hidden), jnp.bfloat16),
            pltpu.VMEM((rows, k), jnp.bfloat16),
            pltpu.VMEM((rows, k), jnp.bfloat16),
        ],
        compiler_params=params(16),
        cost_estimate=COST,
    )(place, tokens, *weights)


def back_project(own, other, weight, place):
    p, q, _, t, hidden = own.shape
    half = p * q * t
    k = weight.shape[0]

    def body(place_ref, own_ref, other_ref, weight_ref, out_ref):
        grad = jnp.concatenate([own_ref[:, :, 1].reshape(half, hidden), other_ref[:, :, 1].reshape(half, hidden)])
        for i in range(k // 256):
            part = pl.ds(i * 256, 256)
            total = contract(grad, weight_ref[part, :], 1, 1)
            for b in range(2 * half // 16):
                start = pl.multiple_of(place_ref[b] * 16, 16)
                out_ref[pl.ds(start, 16), part] = total[16 * b : 16 * b + 16]

    return pl.pallas_call(
        body,
        in_specs=[SMEM, VMEM, VMEM, VMEM],
        out_specs=VMEM,
        out_shape=pltpu.VMEM((2 * half, k), jnp.float32),
        compiler_params=params(16),
        cost_estimate=COST,
    )(place, own, other, weight)


def weight_grad(parts, tokens, which):
    hidden = parts[0].shape[-1]
    rows, k = tokens[0].shape
    chunks = len(tokens)
    steps = hidden // TILE

    def body(*refs):
        part_refs, token_refs, out_ref = refs[: 2 * chunks], refs[2 * chunks : 3 * chunks], refs[3 * chunks]
        made, sems = refs[3 * chunks + 1 :][:2]
        both = jnp.concatenate([ref[...] for ref in token_refs])
        if which == 1:
            turned = refs[-1]
            turned[...] = both.T

        copies = []
        for i in range(steps):
            part = pl.ds(i * TILE, TILE)
            value = jnp.concatenate([ref[:, :, which, :, part].reshape(rows // 2, TILE) for ref in part_refs])
            if which == 0:
                made[i] = bf16(contract(value, both, 0, 0))
                target = out_ref.at[part, :]
            else:
                made[i] = bf16(contract(turned[...], value, 1, 0))
                target = out_ref.at[:, part]
            copies.append(pltpu.make_async_copy(made.at[i], target, sems.at[i]))
            copies[-1].start()
        for copy in copies:
            copy.wait()

    return pl.pallas_call(
        body,
        in_specs=[VMEM] * (3 * chunks),
        out_specs=pl.BlockSpec(memory_space=pl.ANY),
        out_shape=jax.ShapeDtypeStruct((hidden, k) if which == 0 else (k, hidden), jnp.bfloat16),
        scratch_shapes=[
            pltpu.VMEM((steps, TILE, k) if which == 0 else (steps, k, TILE), jnp.bfloat16),
            pltpu.SemaphoreType.DMA((steps,)),
        ]
        + ([] if which == 0 else [pltpu.VMEM((k, chunks * rows), jnp.bfloat16)]),
        compiler_params=params(16),
        cost_estimate=COST,
    )(*parts, *tokens)


def gather_y(a):
    return jnp.stack([a] + [from_row(a, dy, 0, 0) for dy in (1, 2, 3)])


def gather_x(a):
    return jnp.stack([a, from_row(a, 0, 1, 0)])


def gather_z(a):
    return jnp.stack([a] + [from_col(a, 0, dz) for dz in (1, 2, 3)])


def sum_y(part):
    got = [from_row(bf16(part(dy)), -dy, 0, 0) for dy in (1, 3, 2)]
    return part(0) + f32(got[0]) + f32(got[1]) + f32(got[2])


def sum_x(part):
    return part(0) + f32(from_row(bf16(part(1)), 0, 1, 0))


def sum_z(part):
    got = [from_col(bf16(part[dz]), 0, -dz) for dz in (1, 3, 2)]
    return part[0] + f32(got[0]) + f32(got[1]) + f32(got[2])


def tied(a, *others):
    return lax.optimization_barrier((a, *others))[0]


def on_device(inputs, cotangent, weight_in, weight_out):
    n, k = inputs.shape
    row = lax.axis_index("row")
    y, x, c = row // 4, (row // 2) % 2, row % 2

    def place_of(x_outer):
        b = jnp.arange(16, dtype=jnp.int32)
        dc = b // 8
        dx, dy = ((b // 4) % 2, b % 4) if x_outer else (b % 2, (b // 2) % 4)
        return (((y + dy) % 4) * 2 + (c + dc) % 2) * 2 + (x + dx) % 2

    def made_of(sums):
        pre, act_grad = sums
        return jnp.stack([bf16(gelu_value(pre)), bf16(act_grad * gelu_slope(pre))])

    own = jnp.stack([inputs, cotangent])
    near = from_col(own, 1, 0)
    weights = loaded(tied(weight_in, near), weight_out)
    tokens_a = jnp.stack([tied(own, weights[0])] + [from_col(own, 0, dz) for dz in (1, 2, 3)])
    place_a, place_b = place_of(True), place_of(False)
    keep_a, send_a, *placed_a = project(tokens_a, weights, place_a)
    send_a, tokens_b = lax.optimization_barrier((send_a, gather_z(near)))
    pair_a = keep_a + f32(from_row(send_a, 0, 0, 1))
    keep_b, send_b, *placed_b = project(tokens_b, weights, place_b)
    pair_b = keep_b + f32(from_row(send_b, 0, 0, 1))
    pair_a, pair_b = pair_a.reshape(2, 2, 4, 16, -1), pair_b.reshape(2, 4, 2, 16, -1)

    one_a, one_b = sum_y(lambda dy: pair_a[:, :, dy]), sum_x(lambda dx: pair_b[:, :, dx])
    one_a, one_b = lax.optimization_barrier((one_a, one_b))
    sums_b = sum_y(lambda dy: one_b[:, dy])
    sums_a = one_a[:, 0] + f32(tied(from_row(bf16(one_a[:, 1]), 0, 1, 0), sums_b))
    made_a, made_b = made_of(sums_a), made_of(sums_b)
    made_a, made_b = lax.optimization_barrier((made_a, made_b))
    part_a = gather_y(made_a)
    part_b = jnp.stack([made_b, tied(from_row(made_b, 0, 1, 0), part_a)])
    part_a, part_b = lax.optimization_barrier((part_a, part_b))
    half_a, half_b = gather_x(part_a), gather_y(part_b)
    other_b = from_row(half_b, 0, 0, 1)
    back_b = back_project(half_b, other_b, weights[0], place_b).reshape(4, n, k)
    other_a = from_row(half_a, 0, 0, 1)
    back_a = back_project(half_a, other_a, weights[0], place_a).reshape(4, n, k)
    total = sum_z(back_a)
    for dz in (0, 1, 3, 2):
        total = total + f32(from_col(bf16(back_b[dz]), 1, -dz))
    parts = [half_a, other_a, half_b, other_b]
    weight_out_grad = weight_grad(parts, [placed_a[1], placed_b[1]], 0)
    weight_in_grad = weight_grad(parts, [placed_a[0], placed_b[0]], 1)
    return (weight_in_grad, weight_out_grad, bf16(total))


def solution(mesh):
    return jax.shard_map(
        on_device,
        mesh=mesh,
        in_specs=(P("col", "row"), P("col", "row"), P("row", "col"), P("col", "row")),
        out_specs=(P("row", "col"), P("col", "row"), P("col", "row")),
        check_vma=False,
    )
```

```python
import functools
import math

import jax
import jax.numpy as jnp
from jax import lax
from jax.experimental import pallas as pl
from jax.experimental.pallas import tpu as pltpu
from jax.sharding import PartitionSpec as P

ROW = [(y, x, c) for y in range(4) for x in range(2) for c in range(2)]
COL = [(x, z) for x in range(2) for z in range(4)]
MIB = 1 << 20
COST = pl.CostEstimate(flops=1, bytes_accessed=1, transcendentals=0)


def at_row(y, x, c):
    return ((y % 4) * 2 + x % 2) * 2 + c % 2


def at_col(x, z):
    return (x % 2) * 4 + z % 4


def from_row(a, dy, dx, dc):
    return lax.ppermute(a, "row", [(at_row(y + dy, x + dx, c + dc), at_row(y, x, c)) for y, x, c in ROW])


def from_col(a, dx, dz):
    return lax.ppermute(a, "col", [(at_col(x + dx, z + dz), at_col(x, z)) for x, z in COL])


def gelu_value(v):
    inner = math.sqrt(2.0 / math.pi) * (v + 0.044715 * v * v * v)
    return 0.5 * v * (1.0 + jnp.tanh(inner))


def gelu_slope(v):
    coeff = math.sqrt(2.0 / math.pi)
    tanh_part = jnp.tanh(coeff * (v + 0.044715 * v * v * v))
    return 0.5 * (1.0 + tanh_part) + 0.5 * v * (1.0 - tanh_part * tanh_part) * coeff * (
        1.0 + 3.0 * 0.044715 * v * v
    )


def f32(a):
    return a.astype(jnp.float32)


def bf16(a):
    return a.astype(jnp.bfloat16)


def contract(a, b, da, db):
    return lax.dot_general(a, b, (((da,), (db,)), ((), ())), preferred_element_type=jnp.float32)


VMEM = pl.BlockSpec(memory_space=pltpu.VMEM)
SMEM = pl.BlockSpec(memory_space=pltpu.SMEM)
TILE = 512


def params(mib):
    return pltpu.CompilerParams(vmem_limit_bytes=mib * MIB)


def loaded(first, second):
    def body(first_ref, second_ref, first_out, second_out, sems):
        copies = [
            pltpu.make_async_copy(first_ref, first_out, sems.at[0]),
            pltpu.make_async_copy(second_ref, second_out, sems.at[1]),
        ]
        for copy in copies:
            copy.start()
        for copy in copies:
            copy.wait()

    return pl.pallas_call(
        body,
        in_specs=[pl.BlockSpec(memory_space=pl.ANY)] * 2,
        out_specs=[VMEM] * 2,
        out_shape=[pltpu.VMEM(first.shape, first.dtype), pltpu.VMEM(second.shape, second.dtype)],
        scratch_shapes=[pltpu.SemaphoreType.DMA((2,))],
        compiler_params=params(16),
        cost_estimate=COST,
    )(pltpu.with_memory_space_constraint(first, pltpu.HBM), pltpu.with_memory_space_constraint(second, pltpu.HBM))


def project(tokens, weights, place):
    z, _, n, k = tokens.shape
    rows = z * n
    half, hidden = rows // 2, weights[0].shape[1]

    def body(place_ref, tokens_ref, in_ref, out_ref, keep_ref, send_ref, *placed_refs):
        for m, (weight_ref, placed_ref) in enumerate(zip((in_ref, out_ref), placed_refs)):
            for b in range(rows // 16):
                at = place_ref[b]
                start = pl.multiple_of(lax.rem(at, n // 16) * 16, 16)
                placed_ref[pl.ds(16 * b, 16), :] = tokens_ref[lax.div(at, n // 16), m, pl.ds(start, 16), :]
            for i in range(hidden // TILE):
                part = pl.ds(i * TILE, TILE)
                weight_part = weight_ref[part, :] if m else weight_ref[:, part]
                total = contract(placed_ref[...], weight_part, 1, m)
                keep_ref[m, :, part] = total[:half]
                send_ref[m, :, part] = bf16(total[half:])

    return pl.pallas_call(
        body,
        in_specs=[SMEM, VMEM, VMEM, VMEM],
        out_specs=[VMEM] * 4,
        out_shape=[
            pltpu.VMEM((2, half, hidden), jnp.float32),
            pltpu.VMEM((2, half, hidden), jnp.bfloat16),
            pltpu.VMEM((rows, k), jnp.bfloat16),
            pltpu.VMEM((rows, k), jnp.bfloat16),
        ],
        compiler_params=params(16),
        cost_estimate=COST,
    )(place, tokens, *weights)


def back_project(own, other, weight, place):
    p, q, t, hidden = own.shape
    half = p * q * t
    k = weight.shape[0]

    def body(place_ref, own_ref, other_ref, weight_ref, out_ref):
        grad = jnp.concatenate([ref[...].reshape(half, hidden) for ref in (own_ref, other_ref)])
        for i in range(k // 256):
            part = pl.ds(i * 256, 256)
            total = contract(grad, weight_ref[part, :], 1, 1)
            for b in range(2 * half // 16):
                start = pl.multiple_of(place_ref[b] * 16, 16)
                out_ref[pl.ds(start, 16), part] = total[16 * b : 16 * b + 16]

    return pl.pallas_call(
        body,
        in_specs=[SMEM, VMEM, VMEM, VMEM],
        out_specs=VMEM,
        out_shape=pltpu.VMEM((2 * half, k), jnp.float32),
        compiler_params=params(16),
        cost_estimate=COST,
    )(place, own, other, weight)


def weight_grad(parts, tokens, which):
    hidden = parts[0].shape[-1]
    rows, k = tokens[0].shape
    chunks = len(tokens)
    steps = hidden // TILE

    def body(*refs):
        part_refs, token_refs, out_ref = refs[: 2 * chunks], refs[2 * chunks : 3 * chunks], refs[3 * chunks]
        made, sems = refs[3 * chunks + 1 :][:2]
        both = jnp.concatenate([ref[...] for ref in token_refs])
        if which == 1:
            turned = refs[-1]
            turned[...] = both.T

        copies = []
        for i in range(steps):
            part = pl.ds(i * TILE, TILE)
            value = jnp.concatenate([ref[:, :, :, part].reshape(rows // 2, TILE) for ref in part_refs])
            if which == 0:
                made[i] = bf16(contract(value, both, 0, 0))
                target = out_ref.at[part, :]
            else:
                made[i] = bf16(contract(turned[...], value, 1, 0))
                target = out_ref.at[:, part]
            copies.append(pltpu.make_async_copy(made.at[i], target, sems.at[i]))
            copies[-1].start()
        for copy in copies:
            copy.wait()

    return pl.pallas_call(
        body,
        in_specs=[VMEM] * (3 * chunks),
        out_specs=pl.BlockSpec(memory_space=pl.ANY),
        out_shape=jax.ShapeDtypeStruct((hidden, k) if which == 0 else (k, hidden), jnp.bfloat16),
        scratch_shapes=[
            pltpu.VMEM((steps, TILE, k) if which == 0 else (steps, k, TILE), jnp.bfloat16),
            pltpu.SemaphoreType.DMA((steps,)),
        ]
        + ([] if which == 0 else [pltpu.VMEM((k, chunks * rows), jnp.bfloat16)]),
        compiler_params=params(16),
        cost_estimate=COST,
    )(*parts, *tokens)


def gather_y(a):
    return jnp.stack([a] + [from_row(a, dy, 0, 0) for dy in (1, 2, 3)])


def gather_x(a):
    return jnp.stack([a, from_row(a, 0, 1, 0)])


def gather_z(a):
    return jnp.stack([a] + [from_col(a, 0, dz) for dz in (1, 2, 3)])


def sum_y(part):
    got = [from_row(bf16(part(dy)), -dy, 0, 0) for dy in (1, 3, 2)]
    return part(0) + f32(got[0]) + f32(got[1]) + f32(got[2])


def sum_x(part):
    return part(0) + f32(from_row(bf16(part(1)), 0, 1, 0))


def sum_z(part):
    got = [from_col(bf16(part[dz]), 0, -dz) for dz in (1, 3, 2)]
    return part[0] + f32(got[0]) + f32(got[1]) + f32(got[2])


def tied(a, *others):
    return lax.optimization_barrier((a, *others))[0]


def on_device(inputs, cotangent, weight_in, weight_out):
    n, k = inputs.shape
    row = lax.axis_index("row")
    y, x, c = row // 4, (row // 2) % 2, row % 2

    def place_of(x_outer):
        b = jnp.arange(16, dtype=jnp.int32)
        dc = b // 8
        dx, dy = ((b // 4) % 2, b % 4) if x_outer else (b % 2, (b // 2) % 4)
        return (((y + dy) % 4) * 2 + (c + dc) % 2) * 2 + (x + dx) % 2

    def made_of(sums):
        pre, act_grad = sums
        return jnp.stack([bf16(gelu_value(pre)), bf16(act_grad * gelu_slope(pre))])

    own = jnp.stack([inputs, cotangent])
    near = from_col(own, 1, 0)
    weights = loaded(tied(weight_in, near), weight_out)
    tokens_a = jnp.stack([tied(own, weights[0])] + [from_col(own, 0, dz) for dz in (1, 2, 3)])
    place_a, place_b = place_of(True), place_of(False)
    keep_a, send_a, *placed_a = project(tokens_a, weights, place_a)
    send_a, tokens_b = lax.optimization_barrier((send_a, gather_z(near)))
    pair_a = keep_a + f32(from_row(send_a, 0, 0, 1))
    keep_b, send_b, *placed_b = project(tokens_b, weights, place_b)
    pair_b = keep_b + f32(from_row(send_b, 0, 0, 1))
    pair_a, pair_b = pair_a.reshape(2, 2, 4, 16, -1), pair_b.reshape(2, 4, 2, 16, -1)

    one_a, one_b = sum_y(lambda dy: pair_a[:, :, dy]), sum_x(lambda dx: pair_b[:, :, dx])
    one_a, one_b = lax.optimization_barrier((one_a, one_b))
    sums_b = sum_y(lambda dy: one_b[:, dy])
    sums_a = one_a[:, 0] + f32(tied(from_row(bf16(one_a[:, 1]), 0, 1, 0), sums_b))
    made_a, made_b = made_of(sums_a), made_of(sums_b)
    made_a, made_b = lax.optimization_barrier((made_a, made_b))
    part_a = gather_y(made_a)
    part_b = jnp.stack([made_b, tied(from_row(made_b, 0, 1, 0), part_a)])
    part_a, part_b = lax.optimization_barrier((part_a, part_b))
    both_a = [part_a, from_row(part_a, 0, 1, 0)]
    both_b = [part_b] + [from_row(part_b, dy, 0, 0) for dy in (1, 2, 3)]
    (act_a, grad_a), (act_b, grad_b) = (
        [jnp.stack([block[:, m] for block in both]) for m in range(2)] for both in (both_a, both_b)
    )
    grad_other_b = from_row(grad_b, 0, 0, 1)
    back_b = back_project(grad_b, grad_other_b, weights[0], place_b).reshape(4, n, k)
    grad_other_a = from_row(grad_a, 0, 0, 1)
    back_a = back_project(grad_a, grad_other_a, weights[0], place_a).reshape(4, n, k)
    act_other_a, act_other_b = from_row(act_a, 0, 0, 1), from_row(act_b, 0, 0, 1)
    total = sum_z(back_a)
    for dz in (0, 1, 3, 2):
        total = total + f32(from_col(bf16(back_b[dz]), 1, -dz))
    weight_out_grad = weight_grad([act_a, act_other_a, act_b, act_other_b], [placed_a[1], placed_b[1]], 0)
    weight_in_grad = weight_grad([grad_a, grad_other_a, grad_b, grad_other_b], [placed_a[0], placed_b[0]], 1)
    return (weight_in_grad, weight_out_grad, bf16(total))


def solution(mesh):
    return jax.shard_map(
        on_device,
        mesh=mesh,
        in_specs=(P("col", "row"), P("col", "row"), P("row", "col"), P("col", "row")),
        out_specs=(P("row", "col"), P("col", "row"), P("col", "row")),
        check_vma=False,
    )
```

```python
import functools
import math

import jax
import jax.numpy as jnp
from jax import lax
from jax.experimental import pallas as pl
from jax.experimental.pallas import tpu as pltpu
from jax.sharding import PartitionSpec as P

ROW = [(y, x, c) for y in range(4) for x in range(2) for c in range(2)]
COL = [(x, z) for x in range(2) for z in range(4)]
MIB = 1 << 20
COST = pl.CostEstimate(flops=1, bytes_accessed=1, transcendentals=0)


def at_row(y, x, c):
    return ((y % 4) * 2 + x % 2) * 2 + c % 2


def at_col(x, z):
    return (x % 2) * 4 + z % 4


def from_row(a, dy, dx, dc):
    return lax.ppermute(a, "row", [(at_row(y + dy, x + dx, c + dc), at_row(y, x, c)) for y, x, c in ROW])


def from_col(a, dx, dz):
    return lax.ppermute(a, "col", [(at_col(x + dx, z + dz), at_col(x, z)) for x, z in COL])


def gelu_value(v):
    inner = math.sqrt(2.0 / math.pi) * (v + 0.044715 * v * v * v)
    return 0.5 * v * (1.0 + jnp.tanh(inner))


def gelu_slope(v):
    coeff = math.sqrt(2.0 / math.pi)
    tanh_part = jnp.tanh(coeff * (v + 0.044715 * v * v * v))
    return 0.5 * (1.0 + tanh_part) + 0.5 * v * (1.0 - tanh_part * tanh_part) * coeff * (
        1.0 + 3.0 * 0.044715 * v * v
    )


def f32(a):
    return a.astype(jnp.float32)


def bf16(a):
    return a.astype(jnp.bfloat16)


def contract(a, b, da, db):
    return lax.dot_general(a, b, (((da,), (db,)), ((), ())), preferred_element_type=jnp.float32)


VMEM = pl.BlockSpec(memory_space=pltpu.VMEM)
SMEM = pl.BlockSpec(memory_space=pltpu.SMEM)
TILE = 512
GRAD_TILE = 256


def params(mib):
    return pltpu.CompilerParams(vmem_limit_bytes=mib * MIB)


def loaded(first, second):
    def body(first_ref, second_ref, first_out, second_out, sems):
        copies = [
            pltpu.make_async_copy(first_ref, first_out, sems.at[0]),
            pltpu.make_async_copy(second_ref, second_out, sems.at[1]),
        ]
        for copy in copies:
            copy.start()
        for copy in copies:
            copy.wait()

    return pl.pallas_call(
        body,
        in_specs=[pl.BlockSpec(memory_space=pl.ANY)] * 2,
        out_specs=[VMEM] * 2,
        out_shape=[pltpu.VMEM(first.shape, first.dtype), pltpu.VMEM(second.shape, second.dtype)],
        scratch_shapes=[pltpu.SemaphoreType.DMA((2,))],
        compiler_params=params(16),
        cost_estimate=COST,
    )(pltpu.with_memory_space_constraint(first, pltpu.HBM), pltpu.with_memory_space_constraint(second, pltpu.HBM))


def project(tokens, weights, place):
    z, _, n, k = tokens.shape
    rows = z * n
    half, hidden = rows // 2, weights[0].shape[1]

    def body(place_ref, tokens_ref, in_ref, out_ref, keep_ref, send_ref, *placed_refs):
        for m, (weight_ref, placed_ref) in enumerate(zip((in_ref, out_ref), placed_refs)):
            for b in range(rows // 16):
                at = place_ref[b]
                start = pl.multiple_of(lax.rem(at, n // 16) * 16, 16)
                placed_ref[pl.ds(16 * b, 16), :] = tokens_ref[lax.div(at, n // 16), m, pl.ds(start, 16), :]
            for i in range(hidden // TILE):
                part = pl.ds(i * TILE, TILE)
                weight_part = weight_ref[part, :] if m else weight_ref[:, part]
                total = contract(placed_ref[...], weight_part, 1, m)
                keep_ref[m, :, part] = total[:half]
                send_ref[m, :, part] = bf16(total[half:])

    return pl.pallas_call(
        body,
        in_specs=[SMEM, VMEM, VMEM, VMEM],
        out_specs=[VMEM] * 4,
        out_shape=[
            pltpu.VMEM((2, half, hidden), jnp.float32),
            pltpu.VMEM((2, half, hidden), jnp.bfloat16),
            pltpu.VMEM((rows, k), jnp.bfloat16),
            pltpu.VMEM((rows, k), jnp.bfloat16),
        ],
        compiler_params=params(16),
        cost_estimate=COST,
    )(place, tokens, *weights)


def back_project(own, other, weight, place):
    p, q, t, hidden = own.shape
    half = p * q * t
    k = weight.shape[0]

    def body(place_ref, own_ref, other_ref, weight_ref, out_ref):
        grad = jnp.concatenate([ref[...].reshape(half, hidden) for ref in (own_ref, other_ref)])
        for i in range(k // 256):
            part = pl.ds(i * 256, 256)
            total = contract(grad, weight_ref[part, :], 1, 1)
            for b in range(2 * half // 16):
                start = pl.multiple_of(place_ref[b] * 16, 16)
                out_ref[pl.ds(start, 16), part] = total[16 * b : 16 * b + 16]

    return pl.pallas_call(
        body,
        in_specs=[SMEM, VMEM, VMEM, VMEM],
        out_specs=VMEM,
        out_shape=pltpu.VMEM((2 * half, k), jnp.float32),
        compiler_params=params(16),
        cost_estimate=COST,
    )(place, own, other, weight)


def weight_grad(parts, tokens, which):
    hidden = parts[0].shape[-1]
    rows, k = tokens[0].shape
    chunks = len(tokens)
    steps = hidden // GRAD_TILE

    def body(*refs):
        part_refs, token_refs, out_ref = refs[: 2 * chunks], refs[2 * chunks : 3 * chunks], refs[3 * chunks]
        made, sems = refs[3 * chunks + 1 :][:2]
        both = jnp.concatenate([ref[...] for ref in token_refs])
        if which == 1:
            turned = refs[-1]
            turned[...] = both.T

        copies = []
        for i in range(steps):
            part = pl.ds(i * GRAD_TILE, GRAD_TILE)
            value = jnp.concatenate([ref[:, :, :, part].reshape(rows // 2, GRAD_TILE) for ref in part_refs])
            if which == 0:
                made[i] = bf16(contract(value, both, 0, 0))
                target = out_ref.at[part, :]
            else:
                made[i] = bf16(contract(turned[...], value, 1, 0))
                target = out_ref.at[:, part]
            copies.append(pltpu.make_async_copy(made.at[i], target, sems.at[i]))
            copies[-1].start()
        for copy in copies:
            copy.wait()

    return pl.pallas_call(
        body,
        in_specs=[VMEM] * (3 * chunks),
        out_specs=pl.BlockSpec(memory_space=pl.ANY),
        out_shape=jax.ShapeDtypeStruct((hidden, k) if which == 0 else (k, hidden), jnp.bfloat16),
        scratch_shapes=[
            pltpu.VMEM((steps, GRAD_TILE, k) if which == 0 else (steps, k, GRAD_TILE), jnp.bfloat16),
            pltpu.SemaphoreType.DMA((steps,)),
        ]
        + ([] if which == 0 else [pltpu.VMEM((k, chunks * rows), jnp.bfloat16)]),
        compiler_params=params(16),
        cost_estimate=COST,
    )(*parts, *tokens)


def gather_y(a):
    return jnp.stack([a] + [from_row(a, dy, 0, 0) for dy in (1, 2, 3)])


def gather_x(a):
    return jnp.stack([a, from_row(a, 0, 1, 0)])


def gather_z(a):
    return jnp.stack([a] + [from_col(a, 0, dz) for dz in (1, 2, 3)])


def sum_y(part):
    got = [from_row(bf16(part(dy)), -dy, 0, 0) for dy in (1, 3, 2)]
    return part(0) + f32(got[0]) + f32(got[1]) + f32(got[2])


def sum_x(part):
    return part(0) + f32(from_row(bf16(part(1)), 0, 1, 0))


def sum_z(part):
    got = [from_col(bf16(part[dz]), 0, -dz) for dz in (1, 3, 2)]
    return part[0] + f32(got[0]) + f32(got[1]) + f32(got[2])


def tied(a, *others):
    return lax.optimization_barrier((a, *others))[0]


def on_device(inputs, cotangent, weight_in, weight_out):
    n, k = inputs.shape
    row = lax.axis_index("row")
    y, x, c = row // 4, (row // 2) % 2, row % 2

    def place_of(x_outer):
        b = jnp.arange(16, dtype=jnp.int32)
        dc = b // 8
        dx, dy = ((b // 4) % 2, b % 4) if x_outer else (b % 2, (b // 2) % 4)
        return (((y + dy) % 4) * 2 + (c + dc) % 2) * 2 + (x + dx) % 2

    def made_of(sums):
        pre, act_grad = sums
        return jnp.stack([bf16(gelu_value(pre)), bf16(act_grad * gelu_slope(pre))])

    own = jnp.stack([inputs, cotangent])
    near = from_col(own, 1, 0)
    weights = loaded(tied(weight_in, near), weight_out)
    tokens_a = jnp.stack([tied(own, weights[0])] + [from_col(own, 0, dz) for dz in (1, 2, 3)])
    place_a, place_b = place_of(True), place_of(False)
    keep_a, send_a, *placed_a = project(tokens_a, weights, place_a)
    send_a, tokens_b = lax.optimization_barrier((send_a, gather_z(near)))
    pair_a = keep_a + f32(from_row(send_a, 0, 0, 1))
    keep_b, send_b, *placed_b = project(tokens_b, weights, place_b)
    pair_b = keep_b + f32(from_row(send_b, 0, 0, 1))
    pair_a, pair_b = pair_a.reshape(2, 2, 4, 16, -1), pair_b.reshape(2, 4, 2, 16, -1)

    one_a, one_b = sum_y(lambda dy: pair_a[:, :, dy]), sum_x(lambda dx: pair_b[:, :, dx])
    one_a, one_b = lax.optimization_barrier((one_a, one_b))
    sums_b = sum_y(lambda dy: one_b[:, dy])
    sums_a = one_a[:, 0] + f32(tied(from_row(bf16(one_a[:, 1]), 0, 1, 0), sums_b))
    made_a, made_b = made_of(sums_a), made_of(sums_b)
    made_a, made_b = lax.optimization_barrier((made_a, made_b))
    part_a = gather_y(made_a)
    part_b = jnp.stack([made_b, tied(from_row(made_b, 0, 1, 0), part_a)])
    part_a, part_b = lax.optimization_barrier((part_a, part_b))
    both_a = [part_a, from_row(part_a, 0, 1, 0)]
    both_b = [part_b] + [from_row(part_b, dy, 0, 0) for dy in (1, 2, 3)]
    (act_a, grad_a), (act_b, grad_b) = (
        [jnp.stack([block[:, m] for block in both]) for m in range(2)] for both in (both_a, both_b)
    )
    grad_other_b = from_row(grad_b, 0, 0, 1)
    back_b = back_project(grad_b, grad_other_b, weights[0], place_b).reshape(4, n, k)
    grad_other_a = from_row(grad_a, 0, 0, 1)
    back_a = back_project(grad_a, grad_other_a, weights[0], place_a).reshape(4, n, k)
    act_other_a, act_other_b = from_row(act_a, 0, 0, 1), from_row(act_b, 0, 0, 1)
    total = sum_z(back_a)
    for dz in (0, 1, 3, 2):
        total = total + f32(from_col(bf16(back_b[dz]), 1, -dz))
    weight_out_grad = weight_grad([act_a, act_other_a, act_b, act_other_b], [placed_a[1], placed_b[1]], 0)
    weight_in_grad = weight_grad([grad_a, grad_other_a, grad_b, grad_other_b], [placed_a[0], placed_b[0]], 1)
    return (weight_in_grad, weight_out_grad, bf16(total))


def solution(mesh):
    return jax.shard_map(
        on_device,
        mesh=mesh,
        in_specs=(P("col", "row"), P("col", "row"), P("row", "col"), P("col", "row")),
        out_specs=(P("row", "col"), P("col", "row"), P("col", "row")),
        check_vma=False,
    )
```
